32 devices in a mesh: groups: 2 (over y), row: 4 (over z), col: 2 (over x), rep: 2 (over core).
Axes of the slice: x: 2, y: 2, z: 4, core: 2. Of those that a mesh axis runs over, the one named last changes fastest.
Arguments:
- left_blocks: bfloat16 [8, 4, 12, 128, 128], P(('groups', 'row'), ('col', 'rep')), parts along dimension 0, may hold values from -4 to 4
- left_coords: int32 [8, 4, 2, 12], P(('groups', 'row'), ('col', 'rep')), parts along dimension 0, may hold values from -1 to 27, as said below
- right_blocks: bfloat16 [8, 4, 12, 128, 128], P(('groups', 'row'), ('col', 'rep')), parts along dimension 0, may hold values from -4 to 4
- right_coords: int32 [8, 4, 2, 12], P(('groups', 'row'), ('col', 'rep')), parts along dimension 0, may hold values from -1 to 27, as said below
Outputs:
- product: bfloat16 [8192, 4096], P(('groups', 'row'), ('col', 'rep')), parts along dimension 0
The draws below stay inside these ranges and needn't reach their ends.
There are 2 independent parts, one for each index of `groups`. The reference program is written for one: setup_inputs(seed, part) draws one part's arguments, and reference() takes and returns one part's arrays. A program takes and returns all parts, laid end to end along the dimension named above; each array names one. Nothing has to cross between parts.
Inputs may be any that keep to these rules, and one draw needn't show every extreme that they name: `left_coords`: in every tile the live slots come first and hold distinct positions; slots after them have both coordinates -1. Every tile holds at least one live slot and at most 12, and some tile holds exactly 12. `right_coords`: in every tile the live slots come first and hold distinct positions; slots after them have both coordinates -1. Every tile holds at least two live slots and at most 12, some tile exactly 12; no block row of a tile holds more than 2 live slots, and in every tile some block row holds exactly 2.
All inputs are finite; a program needn't handle non-finite values.
Results may differ from the reference program's by a relative error of at most 0.001.
Values may be sent and summed in bfloat16 or wider, within the bound.
No kernel may reach another device: no remote copies, remote signals or barrier semaphores. Data moves between devices by JAX's collectives and lax.ppermute only.
A program may use at most 64 MiB of HBM per device.

```python
import jax
import jax.numpy as jnp
from jax import lax

BS = 128
KB = 28
RB = 8
WR = 2
CAP = 12
GRID = 4


def draw_counts(seed_key, lowest):
    count_key, where_key = jax.random.split(seed_key)
    counted = jax.random.randint(count_key, (GRID * GRID,), lowest, CAP + 1)
    full_tile = jax.random.randint(where_key, (), 0, GRID * GRID)
    return counted.at[full_tile].set(CAP)


def draw_left_coords(key, part):
    key = jax.random.fold_in(key, 11)
    count_key, tile_key = jax.random.split(key)
    counted = draw_counts(count_key, 1)
    tile_seeds = jax.random.split(tile_key, GRID * GRID)

    def one_tile(tile_seed, live_count):
        shuffled = jax.random.permutation(tile_seed, RB * KB)[:CAP]
        is_live = jnp.arange(CAP) < live_count
        row_ids = jnp.where(is_live, shuffled // KB, -1)
        col_ids = jnp.where(is_live, shuffled % KB, -1)
        return jnp.stack([row_ids, col_ids]).astype(jnp.int32)
    return jax.vmap(one_tile)(tile_seeds, counted).reshape(GRID, GRID, 2, CAP)


def draw_right_coords(key, part):
    key = jax.random.fold_in(key, 23)
    count_key, tile_key = jax.random.split(key)
    counted = draw_counts(count_key, 2)
    tile_seeds = jax.random.split(tile_key, GRID * GRID)

    def one_tile(tile_seed, live_count):
        order_key, offset_key = jax.random.split(tile_seed)
        shuffled = jax.random.permutation(order_key, KB * WR)
        first_row = shuffled[0] // WR
        priority = jnp.where(shuffled // WR == first_row, shuffled % WR, WR + jnp.arange(KB * WR))
        shuffled = shuffled[jnp.argsort(priority, stable=True)][:CAP]
        row_ids = shuffled // WR
        within = shuffled % WR
        offsets = jax.random.randint(offset_key, (KB,), 0, RB)
        col_ids = (offsets[row_ids] + within) % RB
        is_live = jnp.arange(CAP) < live_count
        return jnp.stack([jnp.where(is_live, row_ids, -1), jnp.where(is_live, col_ids, -1)]).astype(jnp.int32)
    return jax.vmap(one_tile)(tile_seeds, counted).reshape(GRID, GRID, 2, CAP)


def level_of(stream_key, shape, cuts, least, top_value):
    gain, own = 1.0, jax.random.fold_in(stream_key, 6)
    for dim, parts in cuts:
        draws = jnp.exp(jax.random.uniform(jax.random.fold_in(own, dim), (parts,), jnp.float32, least / len(cuts), top_value / len(cuts)))
        gain = gain * jnp.repeat(draws, shape[dim] // parts).reshape([-1 if axis == dim else 1 for axis in range(len(shape))])
    return gain


def scatter_about(stream_key, shape, deviation, most, cuts=(), held_as=jnp.bfloat16):
    drawn = jax.random.normal(stream_key, shape, jnp.float32) * deviation
    if len(cuts) > 0:
        drawn = level_of(stream_key, shape, cuts, -0.22, 0.18) * drawn
    return jnp.clip(drawn, min=-most, max=most).astype(held_as)


def setup_inputs(seed: int = 0, part: int = 0) -> dict:
    key_of = jax.random.split(jax.random.key(seed), 5)
    part_splits = jax.random.split(jax.random.fold_in(key_of[4], part), 5)
    left_blocks = scatter_about(part_splits[0], (GRID, GRID, CAP, BS, BS), 0.3, 4.0, ((0, 4), (1, 4)))
    left_coords = draw_left_coords(jax.random.fold_in(jax.random.fold_in(key_of[4], part), 71), part)
    right_blocks = scatter_about(part_splits[2], (GRID, GRID, CAP, BS, BS), 0.3, 4.0, ((0, 4), (1, 4)))
    right_coords = draw_right_coords(jax.random.fold_in(jax.random.fold_in(key_of[4], part), 71), part)
    return {"left_blocks": left_blocks, "left_coords": left_coords, "right_blocks": right_blocks, "right_coords": right_coords}


def tile_terms(left_vals, left_pos, right_vals, right_pos):
    slot_count = left_vals.shape[0]
    left_row = left_pos[0]
    left_col = left_pos[1]
    right_row = right_pos[0]
    right_col = right_pos[1]
    matches = (left_col[:, None] == right_row[None, :]) & (left_col[:, None] >= 0) & (right_row[None, :] >= 0)
    ranking = jnp.cumsum(matches.astype(jnp.int32), axis=1)
    levels = jnp.arange(1, WR + 1, dtype=jnp.int32)
    chosen = (matches[:, None, :] & (ranking[:, None, :] == levels[None, :, None])).astype(jnp.int32)
    present = jnp.sum(chosen, axis=2)
    partner = jnp.sum(chosen * jnp.arange(slot_count, dtype=jnp.int32)[None, None, :], axis=2).astype(jnp.int32)
    picked = right_vals[partner]
    products = jnp.einsum("aij,awjk->awik", left_vals.astype(jnp.float32), picked.astype(jnp.float32), precision=lax.Precision.HIGHEST)
    target = left_row[:, None] * RB + right_col[partner]
    is_live = (present > 0) & (left_row[:, None] >= 0)
    places = jnp.arange(RB * RB, dtype=jnp.int32)
    weights = jnp.where(is_live[:, :, None] & (target[:, :, None] == places[None, None, :]), 1.0, 0.0).astype(jnp.float32)
    return products.reshape(slot_count * WR, BS * BS), weights.reshape(slot_count * WR, RB * RB)


def reference(left_blocks, left_coords, right_blocks, right_coords):
    def per_tile(flat_index):
        row_tile = flat_index // GRID
        col_tile = flat_index % GRID

        def accumulate(summed, tile_index):
            products, weights = tile_terms(left_blocks[row_tile, tile_index], left_coords[row_tile, tile_index], right_blocks[tile_index, col_tile], right_coords[tile_index, col_tile])
            return summed + jnp.einsum("pc,pe->ce", weights, products, precision=lax.Precision.HIGHEST), None

        start_sum = jnp.zeros((RB * RB, BS * BS), jnp.float32)
        summed = lax.scan(accumulate, start_sum, jnp.arange(GRID, dtype=jnp.int32))[0]
        return summed.reshape(RB, RB, BS, BS).transpose(0, 2, 1, 3).reshape(RB * BS, RB * BS).astype(jnp.bfloat16)

    all_tiles = lax.map(per_tile, jnp.arange(GRID * GRID, dtype=jnp.int32))
    return all_tiles.reshape(GRID, GRID, RB * BS, RB * BS).transpose(0, 2, 1, 3).reshape(GRID * RB * BS, GRID * RB * BS)
```

```python
import functools

import jax
import jax.numpy as jnp
from jax import lax
from jax.experimental import pallas as pl
from jax.experimental.pallas import tpu as pltpu
from jax.sharding import PartitionSpec as P

BS = 128
RB = 8
KB = 28
TAIL = 16
CR = ("col", "rep")
HBM = pl.BlockSpec(memory_space=pltpu.HBM)
VMEM = pl.BlockSpec(memory_space=pltpu.VMEM)
SMEM = pl.BlockSpec(memory_space=pltpu.SMEM)


def kept(memory, *arrays):
    return [pltpu.with_memory_space_constraint(array, memory) for array in arrays]


def pack_kernel(right, right_pos, left, left_pos, right_out, left_out, pos, sems):
    rows, slots = right.shape[0], right_pos.shape[1]
    copies = [
        pltpu.make_async_copy(right, right_out.at[pl.ds(0, rows)], sems.at[0]),
        pltpu.make_async_copy(left, left_out.at[pl.ds(0, rows)], sems.at[1]),
        pltpu.make_async_copy(right_pos, pos.at[0], sems.at[2]),
        pltpu.make_async_copy(left_pos, pos.at[1], sems.at[3]),
    ]
    for copy in copies:
        copy.start()
    for i, packed in enumerate((right_out, left_out)):
        copies[2 + i].wait()
        tail = jnp.pad(pos[i].astype(jnp.float32), ((0, TAIL - 2), (0, BS - slots)))
        packed[pl.ds(rows, TAIL), :] = tail.astype(jnp.bfloat16)
    for copy in copies[:2]:
        copy.wait()


def pack(right, right_pos, left, left_pos):
    packed = pltpu.VMEM((right.shape[0] + TAIL, BS), jnp.bfloat16)
    return pl.pallas_call(
        pack_kernel,
        out_shape=(packed, packed),
        in_specs=[HBM] * 4,
        out_specs=(VMEM, VMEM),
        scratch_shapes=[
            pltpu.VMEM((2, *right_pos.shape), jnp.int32),
            pltpu.SemaphoreType.DMA((4,)),
        ],
        compiler_params=pltpu.CompilerParams(vmem_limit_bytes=4 * 2**20),
    )(*kept(pltpu.HBM, right, right_pos, left, left_pos))


def block(ref, i):
    return ref[pl.ds(pl.multiple_of(i * BS, BS), BS), :]


def read_tail(ref, rows, whole, i):
    whole[pl.ds(8 * i, 8), :] = ref[pl.ds(rows, TAIL), :][:8].astype(jnp.float32).astype(jnp.int32)


def find_pairs(lc, lp, rc, rp, slots, tab, pairs, count):
    for u in range(slots):
        at = rc[rp, u] + 1
        tab[at] = tab[at] * 32 + (u + 1)
    tab[0] = 0
    for s in range(slots):
        met = tab[lc[lp + 1, s] + 1]
        for which in (met & 31, met >> 5):
            u = jnp.maximum(which - 1, 0)
            place = jnp.maximum(lc[lp, s] * RB + rc[rp + 1, u], 0)
            pairs[count] = ((lp // 8 * slots + s) * slots + u) * 64 + place
            count = count + jnp.minimum(which, 1)
    for u in range(slots):
        tab[rc[rp, u] + 1] = 0
    return count


def add_pairs(pairs, start, end, lall, right, slots, acc, seen, touched, sent):
    def multiply(p, sent):
        pair = pairs[p]
        place = pair & 63
        slot = pair >> 6
        acc[pl.ds(pl.multiple_of(place * BS, BS), BS), :] += jnp.dot(
            block(lall, slot // slots), block(right, slot % slots), preferred_element_type=jnp.float32
        )
        touched[sent] = place
        first = 1 - seen[place]
        seen[place] = 1
        return sent + first

    return lax.fori_loop(start, end, multiply, sent)


def send_blocks(touched, sent, acc, stage, out, sem):
    def block_out(i, place):
        at = (
            pl.ds(pl.multiple_of((place >> 3) * BS, BS), BS),
            pl.ds(pl.multiple_of((place & 7) * BS, BS), BS),
        )
        return pltpu.make_async_copy(stage.at[i], out.at[at], sem)

    def send(i, carry):
        stage[i] = block(acc, touched[i]).astype(jnp.bfloat16)
        block_out(i, touched[i]).start()
        return carry

    def settle(i, carry):
        block_out(0, 0).wait()
        return carry

    lax.fori_loop(0, sent, send, 0)
    lax.fori_loop(0, sent, settle, 0)


def clear_scalars(*refs):
    for ref in refs:
        for i in range(ref.shape[0]):
            ref[i] = 0


def early_kernel(tiles, slots, links, *refs):
    lefts, rights = refs[:tiles], refs[tiles:-13]
    out, acc, lall, lc = refs[-13:-9]
    stage, zeros, whole, coords, tab, pairs, seen, touched, sems = refs[-9:]
    rows = slots * BS

    zeros[...] = jnp.zeros_like(zeros)
    clears = [
        pltpu.make_async_copy(zeros, out.at[pl.ds(i * BS, BS), :], sems.at[0]) for i in range(RB)
    ]
    for clear in clears:
        clear.start()
    for i, ref in enumerate(lefts):
        read_tail(ref, rows, whole, i)
    for b, ref in enumerate(rights):
        read_tail(ref, rows, whole, tiles + b)
    scalars = [
        pltpu.make_async_copy(whole.at[pl.ds(0, 8 * tiles)], lc, sems.at[1]),
        pltpu.make_async_copy(whole.at[pl.ds(8 * tiles, 8 * len(rights))], coords, sems.at[2]),
    ]
    for copy in scalars:
        copy.start()
    clear_scalars(tab, seen)
    for j, ref in enumerate(lefts):
        lall[pl.ds(j * rows, rows), :] = ref[pl.ds(0, rows), :]
    acc[...] = jnp.zeros_like(acc)
    for copy in scalars:
        copy.wait()

    sent = jnp.int32(0)
    for b, ref in enumerate(rights):
        count = find_pairs(lc, 8 * links[b], coords, 8 * b, slots, tab, pairs, jnp.int32(0))
        sent = add_pairs(pairs, 0, count, lall, ref, slots, acc, seen, touched, sent)
    for clear in clears:
        clear.wait()
    send_blocks(touched, sent, acc, stage, out, sems.at[3])


def late_kernel(options, slots, links, late, lc, lall, acc, *refs):
    rights = refs[: sum(options)]
    out, acc_out, stage, whole, coords, tab, pairs, seen, touched, sems = refs[sum(options) + 1 :]
    rows = slots * BS
    groups = []
    for option in options:
        groups.append(rights[:option])
        rights = rights[option:]

    def chosen(group, act):
        if len(group) == 1:
            act(group[0])
        else:
            for choice, ref in enumerate(group):
                pl.when(late[0] == choice)(functools.partial(act, ref))

    for b, group in enumerate(groups):
        chosen(group, lambda ref, b=b: read_tail(ref, rows, whole, b))
    scalars = pltpu.make_async_copy(whole, coords, sems.at[0])
    scalars.start()
    clear_scalars(tab, seen)
    scalars.wait()
    ends = [jnp.int32(0)]
    early = links.shape[0] - len(groups)
    for b in range(len(groups)):
        ends.append(
            find_pairs(lc, 8 * links[early + b], coords, 8 * b, slots, tab, pairs, ends[-1])
        )
    sent = jnp.int32(0)
    for b, group in enumerate(groups):
        for choice, ref in enumerate(group):
            end = ends[b + 1]
            if len(group) > 1:
                end = jnp.where(late[0] == choice, end, ends[b])
            sent = add_pairs(
                pairs, ends[b], end, lall, ref, slots, acc_out, seen, touched, sent
            )
    send_blocks(touched, sent, acc_out, stage, out, sems.at[1])


def multiply_tiles(links, late, lefts, early, later):
    tiles = len(lefts)
    slots = lefts[0].shape[0] // BS
    rows = slots * BS
    product = pltpu.HBM((RB * BS, RB * BS), jnp.bfloat16)
    sums = pltpu.VMEM((RB * RB * BS, BS), jnp.float32)
    scalars = lambda size: pltpu.SMEM((size,), jnp.int32)
    lists = [scalars(KB + 1), scalars(2 * slots * tiles + 8), scalars(RB * RB), scalars(RB * RB + 8)]
    stage = pltpu.VMEM((RB * RB, BS, BS), jnp.bfloat16)
    params = pltpu.CompilerParams(vmem_limit_bytes=8 * 2**20)
    out, acc, lall, lc = pl.pallas_call(
        functools.partial(early_kernel, tiles, slots),
        out_shape=(
            product,
            sums,
            pltpu.VMEM((tiles * rows, BS), jnp.bfloat16),
            pltpu.SMEM((8 * tiles, BS), jnp.int32),
        ),
        in_specs=[SMEM] + [VMEM] * (tiles + len(early)),
        out_specs=(HBM, VMEM, VMEM, SMEM),
        scratch_shapes=[
            stage,
            pltpu.VMEM((BS, RB * BS), jnp.bfloat16),
            pltpu.VMEM((8 * (tiles + len(early)), BS), jnp.int32),
            pltpu.SMEM((8 * len(early), BS), jnp.int32),
            *lists,
            pltpu.SemaphoreType.DMA((4,)),
        ],
        compiler_params=params,
    )(links, *kept(pltpu.VMEM, *lefts, *early))
    options = [len(group) for group in later]
    later = sum(later, [])
    return pl.pallas_call(
        functools.partial(late_kernel, options, slots),
        out_shape=(product, sums),
        in_specs=[SMEM] * 3 + [VMEM] * (2 + len(later)) + [HBM],
        out_specs=(HBM, VMEM),
        scratch_shapes=[
            stage,
            pltpu.VMEM((8 * len(options), BS), jnp.int32),
            pltpu.SMEM((8 * len(options), BS), jnp.int32),
            *lists,
            pltpu.SemaphoreType.DMA((2,)),
        ],
        input_output_aliases={4: 1, 5 + len(later): 0},
        compiler_params=params,
    )(links, late, lc, *kept(pltpu.VMEM, lall, acc, *later), *kept(pltpu.HBM, out))[0]


def shifted(block, axis, distance):
    size = lax.axis_size(axis)
    return lax.ppermute(block, axis, [((i - distance) % size, i) for i in range(size)])


def any_grid(right, left):
    rows, cols = lax.axis_size("row"), lax.axis_size(CR)
    row, col = lax.axis_index("row"), lax.axis_index(CR)
    rights = [right] + [shifted(right, "row", d) for d in range(1, rows)]
    lefts = [left] + [shifted(left, CR, d) for d in range(1, cols)]
    held = (row - jnp.arange(rows)) % rows
    links = (col - held) % cols
    late = jnp.zeros((1,), jnp.int32)
    return links.astype(jnp.int32), late, lefts, rights[:1], [[tile] for tile in rights[1:]]


def line_of_four(right, left):
    row, col = lax.axis_index("row"), lax.axis_index(CR)

    def along(block, route):
        return lax.ppermute(block, "row", route)

    across, swap = [(i, i ^ 2) for i in range(4)], [(i, i ^ 1) for i in range(4)]
    from_far = along(right, [(0, 2), (3, 1)])
    from_mirror = along(right, [(1, 2), (2, 1), (0, 3), (3, 0)])
    from_pair = along(right, [(0, 1), (1, 0), (2, 3), (3, 2)])
    left_x = lax.ppermute(left, CR, across)
    left_c = lax.ppermute(left, CR, swap)
    left_xc = lax.ppermute(left_x, CR, swap)
    relayed = along(from_mirror, [(1, 0), (2, 3)])

    held = jnp.stack([row, 3 - row, row ^ 2, row ^ 1])
    links = held ^ col
    late = jnp.where((row == 0) | (row == 3), 1, 0).astype(jnp.int32).reshape(1)
    lefts = [left, left_c, left_x, left_xc]
    later = [[from_far, relayed], [from_pair]]
    return links.astype(jnp.int32), late, lefts, [right, from_mirror], later


def per_device(left_blocks, left_coords, right_blocks, right_coords):
    grid = (lax.axis_size("row"), lax.axis_size("col"), lax.axis_size("rep"))
    gather = line_of_four if grid == (4, 2, 2) else any_grid
    right, left = pack(
        right_blocks.reshape(-1, BS), right_coords[0, 0], left_blocks.reshape(-1, BS), left_coords[0, 0]
    )
    return multiply_tiles(*gather(right, left))


def solution(mesh):
    return jax.shard_map(
        per_device,
        mesh=mesh,
        in_specs=(
            P(("groups", "row"), CR, None, None, None),
            P(("groups", "row"), CR, None, None),
            P(("groups", "row"), CR, None, None, None),
            P(("groups", "row"), CR, None, None),
        ),
        out_specs=P(("groups", "row"), CR),
        check_vma=False,
    )
```

```python
import functools

import jax
import jax.numpy as jnp
from jax import lax
from jax.experimental import pallas as pl
from jax.experimental.pallas import tpu as pltpu
from jax.sharding import PartitionSpec as P

BS = 128
RB = 8
KB = 28
TAIL = 16
CR = ("col", "rep")
ANY = pl.BlockSpec(memory_space=pl.ANY)
HBM = pl.BlockSpec(memory_space=pltpu.HBM)
VMEM = pl.BlockSpec(memory_space=pltpu.VMEM)
SMEM = pl.BlockSpec(memory_space=pltpu.SMEM)


def kept(memory, *arrays):
    return [pltpu.with_memory_space_constraint(array, memory) for array in arrays]


def pack_kernel(right, right_pos, left, left_pos, right_out, left_out, pos, sems):
    rows, slots = right.shape[0], right_pos.shape[1]
    copies = [
        pltpu.make_async_copy(right, right_out.at[pl.ds(0, rows)], sems.at[0]),
        pltpu.make_async_copy(left, left_out.at[pl.ds(0, rows)], sems.at[1]),
        pltpu.make_async_copy(right_pos, pos.at[0], sems.at[2]),
        pltpu.make_async_copy(left_pos, pos.at[1], sems.at[3]),
    ]
    for copy in copies:
        copy.start()
    for i, packed in enumerate((right_out, left_out)):
        copies[2 + i].wait()
        tail = jnp.pad(pos[i].astype(jnp.float32), ((0, TAIL - 2), (0, BS - slots)))
        packed[pl.ds(rows, TAIL), :] = tail.astype(jnp.bfloat16)
    for copy in copies[:2]:
        copy.wait()


def pack(right, right_pos, left, left_pos):
    packed = pltpu.VMEM((right.shape[0] + TAIL, BS), jnp.bfloat16)
    return pl.pallas_call(
        pack_kernel,
        out_shape=(packed, packed),
        in_specs=[HBM] * 4,
        out_specs=(VMEM, VMEM),
        scratch_shapes=[
            pltpu.VMEM((2, *right_pos.shape), jnp.int32),
            pltpu.SemaphoreType.DMA((4,)),
        ],
        compiler_params=pltpu.CompilerParams(vmem_limit_bytes=4 * 2**20),
    )(*kept(pltpu.HBM, right, right_pos, left, left_pos))


def block(ref, i):
    return ref[pl.ds(pl.multiple_of(i * BS, BS), BS), :]


def read_tail(ref, rows, whole, i):
    whole[pl.ds(8 * i, 8), :] = ref[pl.ds(rows, TAIL), :][:8].astype(jnp.float32).astype(jnp.int32)


def find_pairs(lc, lp, rc, rp, slots, tab, pairs, count):
    for u in range(slots):
        at = rc[rp, u] + 1
        tab[at] = tab[at] * 32 + (u + 1)
    tab[0] = 0
    for s in range(slots):
        met = tab[lc[lp + 1, s] + 1]
        for which in (met & 31, met >> 5):
            u = jnp.maximum(which - 1, 0)
            place = jnp.maximum(lc[lp, s] * RB + rc[rp + 1, u], 0)
            pairs[count] = ((lp // 8 * slots + s) * slots + u) * 64 + place
            count = count + jnp.minimum(which, 1)
    for u in range(slots):
        tab[rc[rp, u] + 1] = 0
    return count


def add_pairs(pairs, start, end, lall, right, slots, acc, seen, touched, sent):
    def multiply(p, sent):
        pair = pairs[p]
        place = pair & 63
        slot = pair >> 6
        acc[pl.ds(pl.multiple_of(place * BS, BS), BS), :] += jnp.dot(
            block(lall, slot // slots), block(right, slot % slots), preferred_element_type=jnp.float32
        )
        touched[sent] = place
        first = 1 - seen[place]
        seen[place] = 1
        return sent + first

    return lax.fori_loop(start, end, multiply, sent)


def send_blocks(touched, sent, acc, stage, out, sem):
    def block_out(i, place):
        at = (
            pl.ds(pl.multiple_of((place >> 3) * BS, BS), BS),
            pl.ds(pl.multiple_of((place & 7) * BS, BS), BS),
        )
        return pltpu.make_async_copy(stage.at[i], out.at[at], sem)

    def send(i, carry):
        stage[i] = block(acc, touched[i]).astype(jnp.bfloat16)
        block_out(i, touched[i]).start()
        return carry

    def settle(i, carry):
        block_out(0, 0).wait()
        return carry

    lax.fori_loop(0, sent, send, 0)
    lax.fori_loop(0, sent, settle, 0)


def clear_scalars(*refs):
    for ref in refs:
        for i in range(ref.shape[0]):
            ref[i] = 0


def early_kernel(tiles, slots, links, late, *refs):
    lefts, rights = refs[:tiles], refs[tiles:-14]
    out, acc, lall, lc = refs[-14:-10]
    ltails, stage, zeros, whole, coords, tab, pairs, seen, touched, sems = refs[-10:]
    rows = slots * BS

    zeros[...] = jnp.zeros_like(zeros)
    clears = [
        pltpu.make_async_copy(zeros, out.at[pl.ds(i * BS, BS), :], sems.at[0]) for i in range(RB)
    ]
    for clear in clears:
        clear.start()
    moves = [
        pltpu.make_async_copy(ref.at[pl.ds(0, rows)], lall.at[pl.ds(j * rows, rows)], sems.at[4])
        for j, ref in enumerate(lefts)
    ]
    tails = [
        pltpu.make_async_copy(ref.at[pl.ds(rows, TAIL)], ltails.at[pl.ds(j * TAIL, TAIL)], sems.at[5])
        for j, ref in enumerate(lefts)
    ]
    for copy in tails + moves:
        copy.start()
    acc[...] = jnp.zeros_like(acc)
    for copy in tails:
        copy.wait()
    for i in range(tiles):
        read_tail(ltails, i * TAIL, whole, i)
    for b, ref in enumerate(rights):
        read_tail(ref, rows, whole, tiles + b)
    scalars = [
        pltpu.make_async_copy(whole.at[pl.ds(0, 8 * tiles)], lc, sems.at[1]),
        pltpu.make_async_copy(whole.at[pl.ds(8 * tiles, 8 * len(rights))], coords, sems.at[2]),
    ]
    for copy in scalars:
        copy.start()
    clear_scalars(tab, seen)
    for copy in scalars + moves:
        copy.wait()
    for b in range(links.shape[0]):
        lc[2, b] = links[b]
    lc[3, 0] = late[0]

    sent = jnp.int32(0)
    for b, ref in enumerate(rights):
        count = find_pairs(lc, 8 * links[b], coords, 8 * b, slots, tab, pairs, jnp.int32(0))
        sent = add_pairs(pairs, 0, count, lall, ref, slots, acc, seen, touched, sent)
    for clear in clears:
        clear.wait()
    send_blocks(touched, sent, acc, stage, out, sems.at[3])


def late_kernel(options, slots, early, lc, lall, acc, *refs):
    rights = refs[: sum(options)]
    out, acc_out, stage, whole, coords, tab, pairs, seen, touched, sems = refs[sum(options) + 1 :]
    rows = slots * BS
    groups = []
    for option in options:
        groups.append(rights[:option])
        rights = rights[option:]

    def chosen(group, act):
        if len(group) == 1:
            act(group[0])
        else:
            for choice, ref in enumerate(group):
                pl.when(lc[3, 0] == choice)(functools.partial(act, ref))

    for b, group in enumerate(groups):
        chosen(group, lambda ref, b=b: read_tail(ref, rows, whole, b))
    scalars = pltpu.make_async_copy(whole, coords, sems.at[0])
    scalars.start()
    clear_scalars(tab, seen)
    scalars.wait()
    ends = [jnp.int32(0)]
    for b in range(len(groups)):
        ends.append(
            find_pairs(lc, 8 * lc[2, early + b], coords, 8 * b, slots, tab, pairs, ends[-1])
        )
    sent = jnp.int32(0)
    for b, group in enumerate(groups):
        for choice, ref in enumerate(group):
            end = ends[b + 1]
            if len(group) > 1:
                end = jnp.where(lc[3, 0] == choice, end, ends[b])
            sent = add_pairs(
                pairs, ends[b], end, lall, ref, slots, acc_out, seen, touched, sent
            )
    send_blocks(touched, sent, acc_out, stage, out, sems.at[1])


def multiply_tiles(links, late, lefts, early, later):
    tiles = len(lefts)
    slots = lefts[0].shape[0] // BS
    rows = slots * BS
    product = pltpu.HBM((RB * BS, RB * BS), jnp.bfloat16)
    sums = pltpu.VMEM((RB * RB * BS, BS), jnp.float32)
    scalars = lambda size: pltpu.SMEM((size,), jnp.int32)
    lists = [scalars(KB + 1), scalars(2 * slots * tiles + 8), scalars(RB * RB), scalars(RB * RB + 8)]
    stage = pltpu.VMEM((RB * RB, BS, BS), jnp.bfloat16)
    params = pltpu.CompilerParams(vmem_limit_bytes=8 * 2**20)
    out, acc, lall, lc = pl.pallas_call(
        functools.partial(early_kernel, tiles, slots),
        out_shape=(
            product,
            sums,
            pltpu.VMEM((tiles * rows, BS), jnp.bfloat16),
            pltpu.SMEM((8 * tiles, BS), jnp.int32),
        ),
        in_specs=[SMEM] * 2 + [ANY] * tiles + [VMEM] * len(early),
        out_specs=(HBM, VMEM, VMEM, SMEM),
        scratch_shapes=[
            pltpu.VMEM((tiles * TAIL, BS), jnp.bfloat16),
            stage,
            pltpu.VMEM((BS, RB * BS), jnp.bfloat16),
            pltpu.VMEM((8 * (tiles + len(early)), BS), jnp.int32),
            pltpu.SMEM((8 * len(early), BS), jnp.int32),
            *lists,
            pltpu.SemaphoreType.DMA((6,)),
        ],
        compiler_params=params,
    )(links, late, lefts[0], *kept(pltpu.HBM, *lefts[1:]), *kept(pltpu.VMEM, *early))
    options = [len(group) for group in later]
    later = sum(later, [])
    return pl.pallas_call(
        functools.partial(late_kernel, options, slots, len(early)),
        out_shape=(product, sums),
        in_specs=[SMEM] + [VMEM] * (2 + len(later)) + [HBM],
        out_specs=(HBM, VMEM),
        scratch_shapes=[
            stage,
            pltpu.VMEM((8 * len(options), BS), jnp.int32),
            pltpu.SMEM((8 * len(options), BS), jnp.int32),
            *lists,
            pltpu.SemaphoreType.DMA((2,)),
        ],
        input_output_aliases={2: 1, 3 + len(later): 0},
        compiler_params=params,
    )(*kept(pltpu.SMEM, lc), *kept(pltpu.VMEM, lall, acc, *later), *kept(pltpu.HBM, out))[0]


def shifted(block, axis, distance):
    size = lax.axis_size(axis)
    return lax.ppermute(block, axis, [((i - distance) % size, i) for i in range(size)])


def any_grid(right, left):
    rows, cols = lax.axis_size("row"), lax.axis_size(CR)
    row, col = lax.axis_index("row"), lax.axis_index(CR)
    rights = [right] + [shifted(right, "row", d) for d in range(1, rows)]
    lefts = [left] + [shifted(left, CR, d) for d in range(1, cols)]
    held = (row - jnp.arange(rows)) % rows
    links = (col - held) % cols
    late = jnp.zeros((1,), jnp.int32)
    return links.astype(jnp.int32), late, lefts, rights[:1], [[tile] for tile in rights[1:]]


def line_of_four(right, left):
    row, col = lax.axis_index("row"), lax.axis_index(CR)

    def along(block, route):
        return lax.ppermute(block, "row", route)

    across, swap = [(i, i ^ 2) for i in range(4)], [(i, i ^ 1) for i in range(4)]
    from_far = along(right, [(0, 2), (3, 1)])
    from_mirror = along(right, [(1, 2), (2, 1), (0, 3), (3, 0)])
    from_pair = along(right, [(0, 1), (1, 0), (2, 3), (3, 2)])
    left_x = lax.ppermute(left, CR, across)
    left_c = lax.ppermute(left, CR, swap)
    left_xc = lax.ppermute(left_x, CR, swap)
    relayed = along(from_mirror, [(1, 0), (2, 3)])

    held = jnp.stack([row, 3 - row, row ^ 1, row ^ 2])
    links = held ^ col
    late = jnp.where((row == 0) | (row == 3), 1, 0).astype(jnp.int32).reshape(1)
    lefts = [left, left_c, left_x, left_xc]
    early = [right, from_mirror, from_pair]
    return links.astype(jnp.int32), late, lefts, early, [[from_far, relayed]]


def per_device(left_blocks, left_coords, right_blocks, right_coords):
    grid = (lax.axis_size("row"), lax.axis_size("col"), lax.axis_size("rep"))
    gather = line_of_four if grid == (4, 2, 2) else any_grid
    right, left = pack(
        right_blocks.reshape(-1, BS), right_coords[0, 0], left_blocks.reshape(-1, BS), left_coords[0, 0]
    )
    return multiply_tiles(*gather(right, left))


def solution(mesh):
    return jax.shard_map(
        per_device,
        mesh=mesh,
        in_specs=(
            P(("groups", "row"), CR, None, None, None),
            P(("groups", "row"), CR, None, None),
            P(("groups", "row"), CR, None, None, None),
            P(("groups", "row"), CR, None, None),
        ),
        out_specs=P(("groups", "row"), CR),
        check_vma=False,
    )
```

```python
import functools

import jax
import jax.numpy as jnp
from jax import lax
from jax.experimental import pallas as pl
from jax.experimental.pallas import tpu as pltpu
from jax.sharding import PartitionSpec as P

BS = 128
RB = 8
KB = 28
TAIL = 16
CR = ("col", "rep")
ANY = pl.BlockSpec(memory_space=pl.ANY)
HBM = pl.BlockSpec(memory_space=pltpu.HBM)
VMEM = pl.BlockSpec(memory_space=pltpu.VMEM)
SMEM = pl.BlockSpec(memory_space=pltpu.SMEM)


def kept(memory, *arrays):
    return [pltpu.with_memory_space_constraint(array, memory) for array in arrays]


def pack_kernel(right, right_pos, left, left_pos, right_out, left_out, pos, sems):
    rows, slots = right.shape[0], right_pos.shape[1]
    copies = [
        pltpu.make_async_copy(right, right_out.at[pl.ds(0, rows)], sems.at[0]),
        pltpu.make_async_copy(left, left_out.at[pl.ds(0, rows)], sems.at[1]),
        pltpu.make_async_copy(right_pos, pos.at[0], sems.at[2]),
        pltpu.make_async_copy(left_pos, pos.at[1], sems.at[3]),
    ]
    for copy in copies:
        copy.start()
    for i, packed in enumerate((right_out, left_out)):
        copies[2 + i].wait()
        tail = jnp.pad(pos[i].astype(jnp.float32), ((0, TAIL - 2), (0, BS - slots)))
        packed[pl.ds(rows, TAIL), :] = tail.astype(jnp.bfloat16)
    for copy in copies[:2]:
        copy.wait()


def pack(right, right_pos, left, left_pos):
    packed = pltpu.VMEM((right.shape[0] + TAIL, BS), jnp.bfloat16)
    return pl.pallas_call(
        pack_kernel,
        out_shape=(packed, packed),
        in_specs=[HBM] * 4,
        out_specs=(VMEM, VMEM),
        scratch_shapes=[
            pltpu.VMEM((2, *right_pos.shape), jnp.int32),
            pltpu.SemaphoreType.DMA((4,)),
        ],
        compiler_params=pltpu.CompilerParams(vmem_limit_bytes=4 * 2**20),
    )(*kept(pltpu.HBM, right, right_pos, left, left_pos))


def block(ref, i):
    return ref[pl.ds(pl.multiple_of(i * BS, BS), BS), :]


def read_tail(ref, rows, whole, i):
    whole[pl.ds(8 * i, 8), :] = ref[pl.ds(rows, TAIL), :][:8].astype(jnp.float32).astype(jnp.int32)


def find_pairs(lc, lp, rc, rp, slots, tab, pairs, count):
    for u in range(slots):
        at = rc[rp, u] + 1
        tab[at] = tab[at] * 32 + (u + 1)
    tab[0] = 0
    for s in range(slots):
        met = tab[lc[lp + 1, s] + 1]
        for which in (met & 31, met >> 5):
            u = jnp.maximum(which - 1, 0)
            place = jnp.maximum(lc[lp, s] * RB + rc[rp + 1, u], 0)
            pairs[count] = ((lp // 8 * slots + s) * slots + u) * 64 + place
            count = count + jnp.minimum(which, 1)
    for u in range(slots):
        tab[rc[rp, u] + 1] = 0
    return count


def add_pairs(pairs, start, end, lall, right, slots, acc, seen, touched, sent):
    def multiply(p, sent):
        pair = pairs[p]
        place = pair & 63
        slot = pair >> 6
        acc[pl.ds(pl.multiple_of(place * BS, BS), BS), :] += jnp.dot(
            block(lall, slot // slots), block(right, slot % slots), preferred_element_type=jnp.float32
        )
        touched[sent] = place
        first = 1 - seen[place]
        seen[place] = 1
        return sent + first

    return lax.fori_loop(start, end, multiply, sent)


def send_blocks(touched, sent, acc, stage, out, sem):
    def block_out(i, place):
        at = (
            pl.ds(pl.multiple_of((place >> 3) * BS, BS), BS),
            pl.ds(pl.multiple_of((place & 7) * BS, BS), BS),
        )
        return pltpu.make_async_copy(stage.at[i], out.at[at], sem)

    def send(i, carry):
        stage[i] = block(acc, touched[i]).astype(jnp.bfloat16)
        block_out(i, touched[i]).start()
        return carry

    def settle(i, carry):
        block_out(0, 0).wait()
        return carry

    lax.fori_loop(0, sent, send, 0)
    lax.fori_loop(0, sent, settle, 0)


def clear_scalars(*refs):
    for ref in refs:
        for i in range(ref.shape[0]):
            ref[i] = 0


def early_kernel(tiles, slots, links, late, *refs):
    lefts, rights = refs[:tiles], refs[tiles:-14]
    out, acc, lall, lc = refs[-14:-10]
    ltails, stage, zeros, whole, coords, tab, pairs, seen, touched, sems = refs[-10:]
    rows = slots * BS

    zeros[...] = jnp.zeros_like(zeros)
    clears = [
        pltpu.make_async_copy(zeros, out.at[pl.ds(i * BS, BS), :], sems.at[0]) for i in range(RB)
    ]
    for clear in clears:
        clear.start()
    moves = [
        pltpu.make_async_copy(ref.at[pl.ds(0, rows)], lall.at[pl.ds(j * rows, rows)], sems.at[4])
        for j, ref in enumerate(lefts)
    ]
    tails = [
        pltpu.make_async_copy(ref.at[pl.ds(rows, TAIL)], ltails.at[pl.ds(j * TAIL, TAIL)], sems.at[5])
        for j, ref in enumerate(lefts)
    ]
    for copy in tails + moves:
        copy.start()
    acc[...] = jnp.zeros_like(acc)
    for copy in tails:
        copy.wait()
    for i in range(tiles):
        read_tail(ltails, i * TAIL, whole, i)
    for b, ref in enumerate(rights):
        read_tail(ref, rows, whole, tiles + b)
    scalars = [
        pltpu.make_async_copy(whole.at[pl.ds(0, 8 * tiles)], lc, sems.at[1]),
        pltpu.make_async_copy(whole.at[pl.ds(8 * tiles, 8 * len(rights))], coords, sems.at[2]),
    ]
    for copy in scalars:
        copy.start()
    clear_scalars(tab, seen)
    for copy in scalars + moves:
        copy.wait()
    for b in range(links.shape[0]):
        lc[2, b] = links[b]
    lc[3, 0] = late[0]

    sent = jnp.int32(0)
    for b, ref in enumerate(rights):
        count = find_pairs(lc, 8 * links[b], coords, 8 * b, slots, tab, pairs, jnp.int32(0))
        sent = add_pairs(pairs, 0, count, lall, ref, slots, acc, seen, touched, sent)
    for clear in clears:
        clear.wait()
    send_blocks(touched, sent, acc, stage, out, sems.at[3])


def late_kernel(when, slots, base, lc, lall, acc, *refs):
    rights = refs[:-11]
    out, acc_out, stage, whole, coords, tab, pairs, seen, touched, sems = refs[-10:]

    def add():
        for b, ref in enumerate(rights):
            read_tail(ref, slots * BS, whole, b)
        scalars = pltpu.make_async_copy(whole, coords, sems.at[0])
        scalars.start()
        clear_scalars(tab, seen)
        scalars.wait()
        sent = jnp.int32(0)
        for b, ref in enumerate(rights):
            count = find_pairs(lc, 8 * lc[2, base + b], coords, 8 * b, slots, tab, pairs, jnp.int32(0))
            sent = add_pairs(pairs, 0, count, lall, ref, slots, acc_out, seen, touched, sent)
        send_blocks(touched, sent, acc_out, stage, out, sems.at[1])

    if when is None:
        add()
    else:
        pl.when(lc[3, 0] == when)(add)


def plan_kernel(when, slots, at, lc, tail, pairs, touched, counts, whole, coords, tab, seen, sems):
    counts[0] = 0
    counts[1] = 0

    @pl.when(lc[3, 0] == when)
    def _():
        read_tail(tail, tail.shape[0] - TAIL, whole, 0)
        scalars = pltpu.make_async_copy(whole, coords, sems.at[0])
        scalars.start()
        clear_scalars(tab, seen)
        scalars.wait()
        count = find_pairs(lc, 8 * lc[2, at], coords, 0, slots, tab, pairs, jnp.int32(0))

        def mark(p, sent):
            place = pairs[p] & 63
            touched[sent] = place
            first = 1 - seen[place]
            seen[place] = 1
            return sent + first

        counts[0] = count
        counts[1] = lax.fori_loop(0, count, mark, jnp.int32(0))


def planned_kernel(slots, pairs, touched, counts, lall, acc, first, rest, out_in, out, acc_out, stage, sems):
    cut = first.shape[0] // BS

    def multiply(p, carry):
        pair = pairs[p]
        slot = pair >> 6
        u = slot % slots

        def add(ref, i):
            acc_out[pl.ds(pl.multiple_of((pair & 63) * BS, BS), BS), :] += jnp.dot(
                block(lall, slot // slots), block(ref, i), preferred_element_type=jnp.float32
            )

        pl.when(u < cut)(lambda: add(first, u))
        pl.when(u >= cut)(lambda: add(rest, u - cut))
        return carry

    lax.fori_loop(0, counts[0], multiply, 0)
    send_blocks(touched, counts[1], acc_out, stage, out, sems.at[0])


def multiply_tiles(links, late, lefts, early, later, planned=None):
    tiles = len(lefts)
    slots = lefts[0].shape[0] // BS
    rows = slots * BS
    product = pltpu.HBM((RB * BS, RB * BS), jnp.bfloat16)
    sums = pltpu.VMEM((RB * RB * BS, BS), jnp.float32)
    scalars = lambda size: pltpu.SMEM((size,), jnp.int32)
    lists = [scalars(KB + 1), scalars(2 * slots * tiles + 8), scalars(RB * RB), scalars(RB * RB + 8)]
    stage = pltpu.VMEM((RB * RB, BS, BS), jnp.bfloat16)
    params = pltpu.CompilerParams(vmem_limit_bytes=8 * 2**20)
    out, acc, lall, lc = pl.pallas_call(
        functools.partial(early_kernel, tiles, slots),
        out_shape=(
            product,
            sums,
            pltpu.VMEM((tiles * rows, BS), jnp.bfloat16),
            pltpu.SMEM((8 * tiles, BS), jnp.int32),
        ),
        in_specs=[SMEM] * 2 + [ANY] * tiles + [VMEM] * len(early),
        out_specs=(HBM, VMEM, VMEM, SMEM),
        scratch_shapes=[
            pltpu.VMEM((tiles * TAIL, BS), jnp.bfloat16),
            stage,
            pltpu.VMEM((BS, RB * BS), jnp.bfloat16),
            pltpu.VMEM((8 * (tiles + len(early)), BS), jnp.int32),
            pltpu.SMEM((8 * len(early), BS), jnp.int32),
            *lists,
            pltpu.SemaphoreType.DMA((6,)),
        ],
        compiler_params=params,
    )(links, late, lefts[0], *kept(pltpu.HBM, *lefts[1:]), *kept(pltpu.VMEM, *early))
    for when, base, tiles_here in later:
        out, acc = pl.pallas_call(
            functools.partial(late_kernel, when, slots, base),
            out_shape=(product, sums),
            in_specs=[SMEM] + [VMEM] * (2 + len(tiles_here)) + [HBM],
            out_specs=(HBM, VMEM),
            scratch_shapes=[
                stage,
                pltpu.VMEM((8 * len(tiles_here), BS), jnp.int32),
                pltpu.SMEM((8 * len(tiles_here), BS), jnp.int32),
                *lists,
                pltpu.SemaphoreType.DMA((2,)),
            ],
            input_output_aliases={2: 1, 3 + len(tiles_here): 0},
            compiler_params=params,
        )(*kept(pltpu.SMEM, lc), *kept(pltpu.VMEM, lall, acc, *tiles_here), *kept(pltpu.HBM, out))
    if planned is None:
        return out
    when, at, first, rest = planned
    short = scalars(2 * slots + 8)
    plan = pl.pallas_call(
        functools.partial(plan_kernel, when, slots, at),
        out_shape=(short, short, scalars(2)),
        in_specs=[SMEM, VMEM],
        out_specs=(SMEM, SMEM, SMEM),
        scratch_shapes=[
            pltpu.VMEM((8, BS), jnp.int32),
            pltpu.SMEM((8, BS), jnp.int32),
            scalars(KB + 1),
            scalars(RB * RB),
            pltpu.SemaphoreType.DMA((1,)),
        ],
        compiler_params=params,
    )(*kept(pltpu.SMEM, lc), *kept(pltpu.VMEM, rest))
    return pl.pallas_call(
        functools.partial(planned_kernel, slots),
        out_shape=(product, sums),
        in_specs=[SMEM] * 3 + [VMEM] * 4 + [HBM],
        out_specs=(HBM, VMEM),
        scratch_shapes=[stage, pltpu.SemaphoreType.DMA((1,))],
        input_output_aliases={4: 1, 7: 0},
        compiler_params=params,
    )(*kept(pltpu.SMEM, *plan), *kept(pltpu.VMEM, lall, acc, first, rest), *kept(pltpu.HBM, out))[0]


def split_kernel(tile, first, rest):
    cut = first.shape[0]
    first[...] = tile[pl.ds(0, cut), :]
    rest[...] = tile[pl.ds(cut, rest.shape[0]), :]


def split(tile, cut):
    return pl.pallas_call(
        split_kernel,
        out_shape=[pltpu.VMEM((n, BS), jnp.bfloat16) for n in (cut, tile.shape[0] - cut)],
        in_specs=[VMEM],
        out_specs=[VMEM, VMEM],
        compiler_params=pltpu.CompilerParams(vmem_limit_bytes=2**20),
    )(*kept(pltpu.VMEM, tile))


def shifted(block, axis, distance):
    size = lax.axis_size(axis)
    return lax.ppermute(block, axis, [((i - distance) % size, i) for i in range(size)])


def tied(block, *others):
    return lax.optimization_barrier((block, *others))[0]


def any_grid(right, left):
    rows, cols = lax.axis_size("row"), lax.axis_size(CR)
    row, col = lax.axis_index("row"), lax.axis_index(CR)
    rights = [right] + [shifted(right, "row", d) for d in range(1, rows)]
    lefts = [left] + [shifted(left, CR, d) for d in range(1, cols)]
    held = (row - jnp.arange(rows)) % rows
    links = (col - held) % cols
    late = jnp.zeros((1,), jnp.int32)
    return links.astype(jnp.int32), late, lefts, rights[:1], [(None, 1, rights[1:])]


def line_of_four(right, left):
    row, col = lax.axis_index("row"), lax.axis_index(CR)

    def along(block, route):
        return lax.ppermute(block, "row", route)

    across, swap = [(i, i ^ 2) for i in range(4)], [(i, i ^ 1) for i in range(4)]
    from_far = along(right, [(0, 2), (3, 1)])
    from_mirror = along(right, [(1, 2), (2, 1), (0, 3), (3, 0)])
    from_pair = along(right, [(0, 1), (1, 0), (2, 3), (3, 2)])
    left_x = lax.ppermute(left, CR, across)
    left_c = lax.ppermute(left, CR, swap)
    left_xc = lax.ppermute(left_x, CR, swap)
    inward = [(1, 0), (2, 3)]
    first, rest = split(from_mirror, 5 * BS)
    relayed = [along(first, inward), along(rest, inward)]

    held = jnp.stack([row, 3 - row, row ^ 1, row ^ 2])
    links = held ^ col
    late = jnp.where((row == 0) | (row == 3), 1, 0).astype(jnp.int32).reshape(1)
    lefts = [left, left_c, left_x, left_xc]
    early = [right, from_mirror, from_pair]
    return links.astype(jnp.int32), late, lefts, early, [(0, 3, [from_far])], (1, 3, *relayed)


def per_device(left_blocks, left_coords, right_blocks, right_coords):
    grid = (lax.axis_size("row"), lax.axis_size("col"), lax.axis_size("rep"))
    gather = line_of_four if grid == (4, 2, 2) else any_grid
    right, left = pack(
        right_blocks.reshape(-1, BS), right_coords[0, 0], left_blocks.reshape(-1, BS), left_coords[0, 0]
    )
    return multiply_tiles(*gather(right, left))


def solution(mesh):
    return jax.shard_map(
        per_device,
        mesh=mesh,
        in_specs=(
            P(("groups", "row"), CR, None, None, None),
            P(("groups", "row"), CR, None, None),
            P(("groups", "row"), CR, None, None, None),
            P(("groups", "row"), CR, None, None),
        ),
        out_specs=P(("groups", "row"), CR),
        check_vma=False,
    )
```

```python
import functools

import jax
import jax.numpy as jnp
from jax import lax
from jax.experimental import pallas as pl
from jax.experimental.pallas import tpu as pltpu
from jax.sharding import PartitionSpec as P

BS = 128
RB = 8
KB = 28
TAIL = 16
CR = ("col", "rep")
ANY = pl.BlockSpec(memory_space=pl.ANY)
HBM = pl.BlockSpec(memory_space=pltpu.HBM)
VMEM = pl.BlockSpec(memory_space=pltpu.VMEM)
SMEM = pl.BlockSpec(memory_space=pltpu.SMEM)


def kept(memory, *arrays):
    return [pltpu.with_memory_space_constraint(array, memory) for array in arrays]


def pack_kernel(right, right_pos, left, left_pos, right_out, left_out, pos, sems):
    rows, slots = right.shape[0], right_pos.shape[1]
    copies = [
        pltpu.make_async_copy(right, right_out.at[pl.ds(0, rows)], sems.at[0]),
        pltpu.make_async_copy(left, left_out.at[pl.ds(0, rows)], sems.at[1]),
        pltpu.make_async_copy(right_pos, pos.at[0], sems.at[2]),
        pltpu.make_async_copy(left_pos, pos.at[1], sems.at[3]),
    ]
    for copy in copies:
        copy.start()
    for i, packed in enumerate((right_out, left_out)):
        copies[2 + i].wait()
        tail = jnp.pad(pos[i].astype(jnp.float32), ((0, TAIL - 2), (0, BS - slots)))
        packed[pl.ds(rows, TAIL), :] = tail.astype(jnp.bfloat16)
    for copy in copies[:2]:
        copy.wait()


def pack(right, right_pos, left, left_pos):
    packed = pltpu.VMEM((right.shape[0] + TAIL, BS), jnp.bfloat16)
    return pl.pallas_call(
        pack_kernel,
        out_shape=(packed, packed),
        in_specs=[HBM] * 4,
        out_specs=(VMEM, VMEM),
        scratch_shapes=[
            pltpu.VMEM((2, *right_pos.shape), jnp.int32),
            pltpu.SemaphoreType.DMA((4,)),
        ],
        compiler_params=pltpu.CompilerParams(vmem_limit_bytes=4 * 2**20),
    )(*kept(pltpu.HBM, right, right_pos, left, left_pos))


def block(ref, i):
    return ref[pl.ds(pl.multiple_of(i * BS, BS), BS), :]


def read_tail(ref, rows, whole, i):
    whole[pl.ds(8 * i, 8), :] = ref[pl.ds(rows, TAIL), :][:8].astype(jnp.float32).astype(jnp.int32)


def find_pairs(lc, lp, rc, rp, slots, tab, pairs, count):
    for u in range(slots):
        at = rc[rp, u] + 1
        tab[at] = tab[at] * 32 + (u + 1)
    tab[0] = 0
    for s in range(slots):
        met = tab[lc[lp + 1, s] + 1]
        for which in (met & 31, met >> 5):
            u = jnp.maximum(which - 1, 0)
            place = jnp.maximum(lc[lp, s] * RB + rc[rp + 1, u], 0)
            pairs[count] = ((lp // 8 * slots + s) * slots + u) * 64 + place
            count = count + jnp.minimum(which, 1)
    for u in range(slots):
        tab[rc[rp, u] + 1] = 0
    return count


def add_pairs(pairs, start, end, lall, right, slots, acc, seen, touched, sent):
    def multiply(p, sent):
        pair = pairs[p]
        place = pair & 63
        slot = pair >> 6
        acc[pl.ds(pl.multiple_of(place * BS, BS), BS), :] += jnp.dot(
            block(lall, slot // slots), block(right, slot % slots), preferred_element_type=jnp.float32
        )
        touched[sent] = place
        first = 1 - seen[place]
        seen[place] = 1
        return sent + first

    return lax.fori_loop(start, end, multiply, sent)


def send_blocks(touched, sent, acc, stage, out, sem):
    def block_out(i, place):
        at = (
            pl.ds(pl.multiple_of((place >> 3) * BS, BS), BS),
            pl.ds(pl.multiple_of((place & 7) * BS, BS), BS),
        )
        return pltpu.make_async_copy(stage.at[i], out.at[at], sem)

    def send(i, carry):
        stage[i] = block(acc, touched[i]).astype(jnp.bfloat16)
        block_out(i, touched[i]).start()
        return carry

    def settle(i, carry):
        block_out(0, 0).wait()
        return carry

    lax.fori_loop(0, sent, send, 0)
    lax.fori_loop(0, sent, settle, 0)


def clear_scalars(*refs):
    for ref in refs:
        for i in range(ref.shape[0]):
            ref[i] = 0


def early_kernel(tiles, slots, links, late, *refs):
    lefts, rights = refs[:tiles], refs[tiles:-14]
    out, acc, lall, lc = refs[-14:-10]
    ltails, stage, zeros, whole, coords, tab, pairs, seen, touched, sems = refs[-10:]
    rows = slots * BS

    zeros[...] = jnp.zeros_like(zeros)
    clears = [
        pltpu.make_async_copy(zeros, out.at[pl.ds(i * BS, BS), :], sems.at[0]) for i in range(RB)
    ]
    for clear in clears:
        clear.start()
    moves = [
        pltpu.make_async_copy(ref.at[pl.ds(0, rows)], lall.at[pl.ds(j * rows, rows)], sems.at[4])
        for j, ref in enumerate(lefts)
    ]
    tails = [
        pltpu.make_async_copy(ref.at[pl.ds(rows, TAIL)], ltails.at[pl.ds(j * TAIL, TAIL)], sems.at[5])
        for j, ref in enumerate(lefts)
    ]
    for copy in tails + moves:
        copy.start()
    acc[...] = jnp.zeros_like(acc)
    for copy in tails:
        copy.wait()
    for i in range(tiles):
        read_tail(ltails, i * TAIL, whole, i)
    for b, ref in enumerate(rights):
        read_tail(ref, rows, whole, tiles + b)
    scalars = [
        pltpu.make_async_copy(whole.at[pl.ds(0, 8 * tiles)], lc, sems.at[1]),
        pltpu.make_async_copy(whole.at[pl.ds(8 * tiles, 8 * len(rights))], coords, sems.at[2]),
    ]
    for copy in scalars:
        copy.start()
    clear_scalars(tab, seen)
    for copy in scalars + moves:
        copy.wait()
    for b in range(links.shape[0]):
        lc[2, b] = links[b]
    lc[3, 0] = late[0]

    sent = jnp.int32(0)
    for b, ref in enumerate(rights):
        count = find_pairs(lc, 8 * links[b], coords, 8 * b, slots, tab, pairs, jnp.int32(0))
        sent = add_pairs(pairs, 0, count, lall, ref, slots, acc, seen, touched, sent)
    for clear in clears:
        clear.wait()
    send_blocks(touched, sent, acc, stage, out, sems.at[3])


def late_kernel(when, slots, base, lc, lall, acc, *refs):
    rights = refs[:-11]
    out, acc_out, stage, whole, coords, tab, pairs, seen, touched, sems = refs[-10:]

    def add():
        for b, ref in enumerate(rights):
            read_tail(ref, slots * BS, whole, b)
        scalars = pltpu.make_async_copy(whole, coords, sems.at[0])
        scalars.start()
        clear_scalars(tab, seen)
        scalars.wait()
        sent = jnp.int32(0)
        for b, ref in enumerate(rights):
            count = find_pairs(lc, 8 * lc[2, base + b], coords, 8 * b, slots, tab, pairs, jnp.int32(0))
            sent = add_pairs(pairs, 0, count, lall, ref, slots, acc_out, seen, touched, sent)
        send_blocks(touched, sent, acc_out, stage, out, sems.at[1])

    if when is None:
        add()
    else:
        pl.when(lc[3, 0] == when)(add)


def first_kernel(when, slots, at, lc, lall, acc, first, out_in, *refs):
    out, acc_out, later, places, counts = refs[:5]
    stage, whole, coords, tab, pairs, seen, touched, sems = refs[5:]
    cut = first.shape[0] // BS
    counts[0] = 0
    counts[1] = 0

    @pl.when(lc[3, 0] == when)
    def _():
        read_tail(first, first.shape[0] - TAIL, whole, 0)
        scalars = pltpu.make_async_copy(whole, coords, sems.at[0])
        scalars.start()
        clear_scalars(tab, seen)
        scalars.wait()
        count = find_pairs(lc, 8 * lc[2, at], coords, 0, slots, tab, pairs, jnp.int32(0))

        def part(p, taken):
            here, there = taken
            pair = pairs[p]
            is_here = jnp.where((pair >> 6) % slots < cut, 1, 0)
            later[there] = pair
            pairs[here] = pair
            return here + is_here, there + 1 - is_here

        here, there = lax.fori_loop(0, count, part, (jnp.int32(0), jnp.int32(0)))
        sent = add_pairs(pairs, 0, here, lall, first, slots, acc_out, seen, touched, jnp.int32(0))
        send_blocks(touched, sent, acc_out, stage, out, sems.at[1])
        clear_scalars(seen)

        def mark(p, sent):
            place = later[p] & 63
            places[sent] = place
            new = 1 - seen[place]
            seen[place] = 1
            return sent + new

        counts[0] = there
        counts[1] = lax.fori_loop(0, there, mark, jnp.int32(0))


def rest_kernel(slots, pairs, places, counts, lall, acc, rest, out_in, out, acc_out, stage, sems):
    cut = slots - rest.shape[0] // BS

    def multiply(p, carry):
        pair = pairs[p]
        slot = pair >> 6
        acc_out[pl.ds(pl.multiple_of((pair & 63) * BS, BS), BS), :] += jnp.dot(
            block(lall, slot // slots),
            block(rest, slot % slots - cut),
            preferred_element_type=jnp.float32,
        )
        return carry

    lax.fori_loop(0, counts[0], multiply, 0)
    send_blocks(places, counts[1], acc_out, stage, out, sems.at[0])


def multiply_tiles(links, late, lefts, early, later, planned=None):
    tiles = len(lefts)
    slots = lefts[0].shape[0] // BS
    rows = slots * BS
    product = pltpu.HBM((RB * BS, RB * BS), jnp.bfloat16)
    sums = pltpu.VMEM((RB * RB * BS, BS), jnp.float32)
    scalars = lambda size: pltpu.SMEM((size,), jnp.int32)
    lists = [scalars(KB + 1), scalars(2 * slots * tiles + 8), scalars(RB * RB), scalars(RB * RB + 8)]
    stage = pltpu.VMEM((RB * RB, BS, BS), jnp.bfloat16)
    params = pltpu.CompilerParams(vmem_limit_bytes=8 * 2**20)
    out, acc, lall, lc = pl.pallas_call(
        functools.partial(early_kernel, tiles, slots),
        out_shape=(
            product,
            sums,
            pltpu.VMEM((tiles * rows, BS), jnp.bfloat16),
            pltpu.SMEM((8 * tiles, BS), jnp.int32),
        ),
        in_specs=[SMEM] * 2 + [ANY] * tiles + [VMEM] * len(early),
        out_specs=(HBM, VMEM, VMEM, SMEM),
        scratch_shapes=[
            pltpu.VMEM((tiles * TAIL, BS), jnp.bfloat16),
            stage,
            pltpu.VMEM((BS, RB * BS), jnp.bfloat16),
            pltpu.VMEM((8 * (tiles + len(early)), BS), jnp.int32),
            pltpu.SMEM((8 * len(early), BS), jnp.int32),
            *lists,
            pltpu.SemaphoreType.DMA((6,)),
        ],
        compiler_params=params,
    )(links, late, lefts[0], *kept(pltpu.HBM, *lefts[1:]), *kept(pltpu.VMEM, *early))
    if planned is not None:
        when, at, first, rest = planned
        short = scalars(2 * slots + 8)
        out, acc, *plan = pl.pallas_call(
            functools.partial(first_kernel, when, slots, at),
            out_shape=(product, sums, short, short, scalars(2)),
            in_specs=[SMEM] + [VMEM] * 3 + [HBM],
            out_specs=(HBM, VMEM, SMEM, SMEM, SMEM),
            scratch_shapes=[
                stage,
                pltpu.VMEM((8, BS), jnp.int32),
                pltpu.SMEM((8, BS), jnp.int32),
                *lists,
                pltpu.SemaphoreType.DMA((2,)),
            ],
            input_output_aliases={2: 1, 4: 0},
            compiler_params=params,
        )(*kept(pltpu.SMEM, lc), *kept(pltpu.VMEM, lall, acc, first), *kept(pltpu.HBM, out))
    for when, base, tiles_here in later:
        out, acc = pl.pallas_call(
            functools.partial(late_kernel, when, slots, base),
            out_shape=(product, sums),
            in_specs=[SMEM] + [VMEM] * (2 + len(tiles_here)) + [HBM],
            out_specs=(HBM, VMEM),
            scratch_shapes=[
                stage,
                pltpu.VMEM((8 * len(tiles_here), BS), jnp.int32),
                pltpu.SMEM((8 * len(tiles_here), BS), jnp.int32),
                *lists,
                pltpu.SemaphoreType.DMA((2,)),
            ],
            input_output_aliases={2: 1, 3 + len(tiles_here): 0},
            compiler_params=params,
        )(*kept(pltpu.SMEM, lc), *kept(pltpu.VMEM, lall, acc, *tiles_here), *kept(pltpu.HBM, out))
    if planned is None:
        return out
    return pl.pallas_call(
        functools.partial(rest_kernel, slots),
        out_shape=(product, sums),
        in_specs=[SMEM] * 3 + [VMEM] * 3 + [HBM],
        out_specs=(HBM, VMEM),
        scratch_shapes=[stage, pltpu.SemaphoreType.DMA((1,))],
        input_output_aliases={4: 1, 6: 0},
        compiler_params=params,
    )(*kept(pltpu.SMEM, *plan), *kept(pltpu.VMEM, lall, acc, rest), *kept(pltpu.HBM, out))[0]


def split_kernel(tile, first, rest):
    cut, rows = first.shape[0] - TAIL, tile.shape[0] - TAIL
    first[pl.ds(0, cut), :] = tile[pl.ds(0, cut), :]
    first[pl.ds(cut, TAIL), :] = tile[pl.ds(rows, TAIL), :]
    rest[...] = tile[pl.ds(cut, rows - cut), :]


def split(tile, cut):
    rows = tile.shape[0] - TAIL
    return pl.pallas_call(
        split_kernel,
        out_shape=[pltpu.VMEM((n, BS), jnp.bfloat16) for n in (cut + TAIL, rows - cut)],
        in_specs=[VMEM],
        out_specs=[VMEM, VMEM],
        compiler_params=pltpu.CompilerParams(vmem_limit_bytes=2**20),
    )(*kept(pltpu.VMEM, tile))


def shifted(block, axis, distance):
    size = lax.axis_size(axis)
    return lax.ppermute(block, axis, [((i - distance) % size, i) for i in range(size)])


def tied(block, *others):
    return lax.optimization_barrier((block, *others))[0]


def any_grid(right, left):
    rows, cols = lax.axis_size("row"), lax.axis_size(CR)
    row, col = lax.axis_index("row"), lax.axis_index(CR)
    rights = [right] + [shifted(right, "row", d) for d in range(1, rows)]
    lefts = [left] + [shifted(left, CR, d) for d in range(1, cols)]
    held = (row - jnp.arange(rows)) % rows
    links = (col - held) % cols
    late = jnp.zeros((1,), jnp.int32)
    return links.astype(jnp.int32), late, lefts, rights[:1], [(None, 1, rights[1:])]


def line_of_four(right, left):
    row, col = lax.axis_index("row"), lax.axis_index(CR)

    def along(block, route):
        return lax.ppermute(block, "row", route)

    across, swap = [(i, i ^ 2) for i in range(4)], [(i, i ^ 1) for i in range(4)]
    from_far = along(right, [(0, 2), (3, 1)])
    from_mirror = along(right, [(1, 2), (2, 1), (0, 3), (3, 0)])
    from_pair = along(right, [(0, 1), (1, 0), (2, 3), (3, 2)])
    left_x = lax.ppermute(left, CR, across)
    left_c = lax.ppermute(left, CR, swap)
    left_xc = lax.ppermute(left_x, CR, swap)
    inward = [(1, 0), (2, 3)]
    first, rest = split(from_mirror, 8 * BS)
    relayed = [along(first, inward), along(rest, inward)]

    held = jnp.stack([row, 3 - row, row ^ 1, row ^ 2])
    links = held ^ col
    late = jnp.where((row == 0) | (row == 3), 1, 0).astype(jnp.int32).reshape(1)
    lefts = [left, left_c, left_x, left_xc]
    early = [right, from_mirror, from_pair]
    return links.astype(jnp.int32), late, lefts, early, [(0, 3, [from_far])], (1, 3, *relayed)


def per_device(left_blocks, left_coords, right_blocks, right_coords):
    grid = (lax.axis_size("row"), lax.axis_size("col"), lax.axis_size("rep"))
    gather = line_of_four if grid == (4, 2, 2) else any_grid
    right, left = pack(
        right_blocks.reshape(-1, BS), right_coords[0, 0], left_blocks.reshape(-1, BS), left_coords[0, 0]
    )
    return multiply_tiles(*gather(right, left))


def solution(mesh):
    return jax.shard_map(
        per_device,
        mesh=mesh,
        in_specs=(
            P(("groups", "row"), CR, None, None, None),
            P(("groups", "row"), CR, None, None),
            P(("groups", "row"), CR, None, None, None),
            P(("groups", "row"), CR, None, None),
        ),
        out_specs=P(("groups", "row"), CR),
        check_vma=False,
    )
```
